32 devices in a mesh: groups: 2 (over y), row: 8 (over z, x), col: 2 (over core).
Axes of the slice: x: 2, y: 2, z: 4, core: 2. Of those that a mesh axis runs over, the one named last changes fastest.
Arguments:
- embeddings: bfloat16 [2048, 512], P(('groups', 'col', 'row')), parts along dimension 0, may hold values from -15 to 15
- noise: float32 [2048], P(('groups', 'col', 'row')), parts along dimension 0, may hold values from 0.5 to 2
- targets: float32 [16, 2048], P(None, ('groups', 'col', 'row')), parts along dimension 1, may hold values from -6 to 6
Outputs:
- weights_out: float32 [16, 2048], P(None, ('groups', 'col', 'row')), parts along dimension 1
- residual: float32 [16, 2048], P(None, ('groups', 'col', 'row')), parts along dimension 1
The draws below stay inside these ranges and needn't reach their ends.
There are 2 independent parts, one for each index of `groups`. The reference program is written for one: setup_inputs(seed, part) draws one part's arguments, and reference() takes and returns one part's arrays. A program takes and returns all parts, laid end to end along the dimension named above; each array names one. Nothing has to cross between parts.
All inputs are finite; a program needn't handle non-finite values.
Results may differ from the reference program's by a relative error of at most 0.00065.
Values may be sent and summed in bfloat16 or wider, within the bound.
A program may use at most 64 MiB of HBM per device.

```python
import math
import jax
import jax.numpy as jnp
from jax import lax

D = 512
LAYERS = 5
ITERS = 2
COLS = 16
N = 1024


def draw_embeddings(key, part):
    key = jax.random.fold_in(key, 7)
    keys = jax.random.split(key, 8)
    count = max(N // 64, 2)
    families = 8
    members = jax.random.randint(keys[0], (N,), 0, count)
    family_vectors = jnp.clip(jax.random.normal(keys[1], (families, D), jnp.float32), -4.0, 4.0)
    own_parts = jnp.clip(jax.random.normal(keys[2], (count, D), jnp.float32), -4.0, 4.0)
    labels = jnp.arange(count)
    family_of = labels % families
    signs = 1.0 - 2.0 * (labels // families % 2).astype(jnp.float32)
    centres = 0.6 * signs[:, None] * family_vectors[family_of] + 0.8 * own_parts
    sample_spread = jnp.exp(jax.random.uniform(keys[3], (N, 1), jnp.float32, jnp.log(0.05), jnp.log(2.0)))
    cluster_spread = jnp.exp(jax.random.uniform(keys[4], (count, 1), jnp.float32, jnp.log(0.5), jnp.log(2.0)))
    spread = sample_spread * cluster_spread[members]
    offsets = jnp.clip(jax.random.normal(keys[5], (N, D), jnp.float32), -5.0, 5.0)
    values = (centres[members] + spread * offsets) / jnp.sqrt(1.0 + spread * spread)
    values = jnp.clip(values, -5.0, 5.0)
    scales = jnp.exp(jax.random.uniform(keys[7], (N, 1), jnp.float32, jnp.log(0.5), jnp.log(3.0)))
    return (values * scales).astype(jnp.bfloat16)


def levels(key, shape, cuts, low, top_value):
    level, own = 1.0, jax.random.fold_in(key, 6)
    for position, blocks in cuts:
        heights = jnp.exp(jax.random.uniform(jax.random.fold_in(own, position), (blocks,), jnp.float32, low / len(cuts), top_value / len(cuts)))
        level = level * jnp.repeat(heights, shape[position] // blocks).reshape([-1 if axis == position else 1 for axis in range(len(shape))])
    return level


def gaussian(stream_key, shape, width, limit, cuts=(), held_as=jnp.bfloat16):
    values = width * jax.random.normal(stream_key, shape, jnp.float32)
    if cuts:
        values = values * levels(stream_key, shape, cuts, -0.22, 0.18)
    return jnp.clip(values, -limit, limit).astype(held_as)


def setup_inputs(seed: int = 0, part: int = 0) -> dict:
    streams_of = jax.random.split(jax.random.key(seed), 4)
    part_keys = jax.random.split(jax.random.fold_in(streams_of[3], part), 4)
    embeddings = draw_embeddings(jax.random.fold_in(jax.random.fold_in(streams_of[3], part), 71), part)
    noise = jnp.clip(jnp.exp(math.log(2.0) - 1.3862944 * jax.random.uniform(part_keys[1], (N,), jnp.float32) ** levels(part_keys[1], (N,), ((0, 16),), -0.2, 0.2)), 0.5, 2.0)
    targets = gaussian(part_keys[2], (COLS, N), 1.0, 6.0, ((1, 16),), jnp.float32)
    return dict(embeddings=embeddings, noise=noise, targets=targets)


def sample_norms(block):
    values = block.astype(jnp.float32)
    return lax.optimization_barrier(jnp.mean(values * values, axis=1)) + 1e-05

def kernel_block(left, right, left_norms, right_norms):
    sigma = jnp.dot(left, right.T, preferred_element_type=jnp.float32) / left.shape[1]
    scale = jnp.sqrt(left_norms[:, None] * right_norms[None, :])
    kernel = sigma
    for layer in range(LAYERS - 1):
        rho = jnp.clip(sigma / scale, -1.0, 1.0)
        angle = jnp.arccos(rho)
        sine = jnp.sqrt(jnp.maximum(1.0 - rho * rho, 0.0))
        sigma = scale / jnp.pi * (sine + (jnp.pi - angle) * rho)
        kernel = sigma + kernel * (jnp.pi - angle) / jnp.pi
    return kernel / LAYERS

def reference(embeddings, noise, targets):
    all_norms = sample_norms(embeddings)
    blocks = 16
    stacked = embeddings.reshape(blocks, N // blocks, D)
    stacked_norms = all_norms.reshape(blocks, N // blocks)

    def apply(vector):

        def one_block(pair):
            block, block_norms = pair
            gram = kernel_block(block, embeddings, block_norms, all_norms)
            return jnp.dot(gram, vector.T, precision=lax.Precision.HIGHEST)
        product = lax.map(one_block, (stacked, stacked_norms)).reshape(N, COLS).T
        return product + noise[None, :] * vector
    weights_out = jnp.zeros_like(targets)
    residual = targets
    direction = targets
    norm_now = lax.optimization_barrier(jnp.sum(residual * residual, axis=1, keepdims=True))
    for step in range(ITERS):
        image = apply(direction)
        alpha = norm_now / lax.optimization_barrier(jnp.sum(direction * image, axis=1, keepdims=True))
        weights_out = weights_out + alpha * direction
        residual = residual - alpha * image
        norm_next = lax.optimization_barrier(jnp.sum(residual * residual, axis=1, keepdims=True))
        direction = residual + norm_next / norm_now * direction
        norm_now = norm_next
    return (weights_out, residual)
```

```python
import functools
import math

import jax
import jax.numpy as jnp
from jax import lax
from jax.experimental import pallas as pl
from jax.experimental.pallas import tpu as pltpu
from jax.sharding import PartitionSpec as P

LAYERS = 5
MESH = pl.DeviceIdType.MESH
ARCCOS = (
    1.5707963050,
    -0.2145988016,
    0.0889789874,
    -0.0501743046,
    0.0308918810,
    -0.0170881256,
    0.0066700901,
    -0.0012624911,
)


def root(x):
    return x * lax.rsqrt(jnp.maximum(x, 1e-30))


def arccos_over_pi(x, root_one_minus):
    total = jnp.full_like(x, ARCCOS[-1] / math.pi)
    for coefficient in ARCCOS[-2::-1]:
        total = total * x + coefficient / math.pi
    return total * root_one_minus


def layers(first):
    rho = jnp.clip(first, -1.0, 1.0)
    kernel = first
    for layer in range(LAYERS - 1):
        size = jnp.abs(rho) if layer == 0 else rho
        rest = 1.0 - size
        angle = arccos_over_pi(size, root(rest))
        share = 1.0 - angle
        if layer == 0:
            share = jnp.where(rho < 0.0, angle, share)
        sigma = root(rest * (1.0 + size)) * (1.0 / math.pi) + share * rho
        kernel = sigma + kernel * share
        rho = jnp.minimum(sigma, 1.0)
    return kernel


def body(
    rows, e_ref, noise_ref, t_ref, w_ref, res_ref,
    ecol, erow, tsib, tall, khi, klo, part, psib, fall, vbuf, cbuf,
    e_send, e_recv, es_send, es_recv, ts_send, ts_recv, t_send, t_recv,
    p_send, p_recv, f_send, f_recv, c_send, c_recv,
):
    f32, bf16 = jnp.float32, jnp.bfloat16
    g, r, c = lax.axis_index("groups"), lax.axis_index("row"), lax.axis_index("col")
    per, width = e_ref.shape
    count = t_ref.shape[0]
    other = 1 - c
    sibling = (g, r, other)
    half = rows // 2
    partner = r + 1 - 2 * lax.rem(r, 2)
    mine = pl.ds(pl.multiple_of(c * per, per), per)

    def copy(src, dst, send, recv, device):
        return pltpu.make_async_remote_copy(
            src_ref=src, dst_ref=dst, send_sem=send, recv_sem=recv, device_id=device, device_id_type=MESH
        )

    def row_peer(k):
        return lax.rem(r + k, rows)

    barrier = pltpu.get_barrier_semaphore()
    for k in range(rows):
        for d in range(2):
            if k or d:
                pl.semaphore_signal(
                    barrier, inc=1, device_id=(g, row_peer(k), lax.rem(c + d, 2)), device_id_type=MESH
                )
    pl.semaphore_wait(barrier, 2 * rows - 1)

    sends = []

    def start(*args):
        one = copy(*args)
        one.start()
        sends.append(one)
        return one

    e_sibling = start(e_ref, erow.at[mine], es_send, es_recv, sibling)
    t_sibling = start(t_ref, tsib, ts_send, ts_recv, sibling)
    start(e_ref, ecol.at[r], e_send.at[0], e_recv.at[r], (g, partner, c))
    for k in range(1, half):
        start(e_ref, ecol.at[r], e_send.at[k], e_recv.at[r], (g, row_peer(2 * k), c))

    ecol[r] = e_ref[...]
    erow[mine, :] = e_ref[...]
    first = c == 0
    lane = lax.broadcasted_iota(jnp.int32, (count, 2 * per), 1)
    row = lax.broadcasted_iota(jnp.int32, (count, 2 * per), 0)

    def pick(x):
        return jnp.where(first, x[:, :per], x[:, per:])

    t_sibling.wait_recv()
    t_mine, t_other = t_ref[...], tsib[...]
    tall[r] = jnp.where(
        first, jnp.concatenate([t_mine, t_other], axis=1), jnp.concatenate([t_other, t_mine], axis=1)
    )
    for k in range(1, rows):
        start(tall.at[r], tall.at[r], t_send.at[k], t_recv.at[r], (g, row_peer(k), c))
    noise = noise_ref[...]
    empty = jnp.zeros_like(noise)
    noise = jnp.where(
        first, jnp.concatenate([noise, empty], axis=1), jnp.concatenate([empty, noise], axis=1)
    )

    e_sibling.wait_recv()
    dims = (((1,), (1,)), ((), ()))
    block = erow[...]
    square = lax.dot_general(block, block, dims, preferred_element_type=f32)
    at = lax.broadcasted_iota(jnp.int32, square.shape, 0) == lax.broadcasted_iota(jnp.int32, square.shape, 1)
    row_norms = jnp.sum(jnp.where(at, square, 0.0), axis=0, keepdims=True) / width + 1e-05
    row_inverse = lax.rsqrt(row_norms)
    row_scale = row_norms * row_inverse / LAYERS
    row_inverse = row_inverse / width

    def gram(s):
        piece = ecol[s]
        sigma = lax.dot_general(piece, erow[...], dims, preferred_element_type=f32)
        wide = piece.astype(f32)
        norms = jnp.sum(wide * wide, axis=1, keepdims=True) / width + 1e-05
        inverse = lax.rsqrt(norms)
        kernel = layers(sigma * inverse * row_inverse)
        kernel = kernel * (norms * inverse) * row_scale
        high = kernel.astype(bf16)
        place = pl.ds(pl.multiple_of(s * per, per), per)
        khi[place, :] = high
        klo[place, :] = (kernel - high.astype(f32)).astype(bf16)

    def arrived(s):
        copy(e_ref, ecol.at[s], e_send.at[0], e_recv.at[s], (g, partner, c)).wait_recv()

    gram(r)
    arrived(partner)
    gram(partner)
    for k in range(1, half):
        s = row_peer(rows - 2 * k)
        arrived(s)
        start(ecol.at[s], ecol.at[s], e_send.at[half + k], e_recv.at[s], (g, partner, c))
        gram(s)
    for k in range(1, half):
        s = lax.rem(partner + rows - 2 * k, rows)
        arrived(s)
        gram(s)

    for k in range(1, rows):
        s = row_peer(k)
        copy(tall.at[r], tall.at[s], t_send.at[k], t_recv.at[s], (g, s, c)).wait_recv()

    def columns(vector):
        for k in range(half):
            a, b = vector[2 * k], vector[2 * k + 1]
            a = jnp.where(first, a, pltpu.roll(a, per, 1))
            b = jnp.where(first, pltpu.roll(b, per, 1), b)
            vbuf[:, 2 * per * k : 2 * per * (k + 1)] = jnp.where(lane < per, a, b)

    def apply(own):
        v = vbuf[...]
        high = v.astype(bf16)
        low = (v - high.astype(f32)).astype(bf16)
        both = jnp.concatenate([high, low], axis=0)
        a = jnp.dot(both, khi[...], preferred_element_type=f32)
        b = jnp.dot(high, klo[...], preferred_element_type=f32)
        return a[:count] + a[count:] + b + noise * own

    def total(x):
        return jnp.sum(jnp.sum(x, axis=0), axis=1, keepdims=True)

    targets = tall[...]
    columns(targets)
    own_targets = tall[r]
    mine_part = apply(own_targets)
    part[0] = mine_part
    p_one = start(part.at[0], psib.at[0], p_send.at[0], p_recv.at[0], sibling)
    p_one.wait_recv()
    fall[r] = mine_part + psib[0]
    for k in range(1, rows):
        start(fall.at[r], fall.at[r], f_send.at[k], f_recv.at[r], (g, row_peer(k), c))
    norm_zero = total(targets * targets)
    for k in range(1, rows):
        s = row_peer(k)
        copy(fall.at[r], fall.at[s], f_send.at[k], f_recv.at[s], (g, s, c)).wait_recv()
    image = fall[...]
    alpha = norm_zero / total(targets * image)
    residual = targets - alpha[None] * image
    norm_one = total(residual * residual)
    beta = norm_one / norm_zero

    columns(residual + beta[None] * targets)
    own_residual = own_targets - alpha * fall[r]
    own_direction = own_residual + beta * own_targets
    mine_part = apply(own_direction)
    part[1] = mine_part
    p_two = start(part.at[1], psib.at[1], p_send.at[1], p_recv.at[1], sibling)
    curve = jnp.sum(own_direction * mine_part, axis=1, keepdims=True)
    me = 2 * r + c
    cbuf[me] = jnp.sum(jnp.where(lane == row, curve, 0.0), axis=0, keepdims=True)
    for k in range(rows):
        for d in range(2):
            if k or d:
                start(
                    cbuf.at[me], cbuf.at[me], c_send.at[2 * k + d], c_recv.at[me],
                    (g, row_peer(k), lax.rem(c + d, 2)),
                )
    p_two.wait_recv()
    image = mine_part + psib[1]
    for k in range(rows):
        for d in range(2):
            if k or d:
                s = 2 * row_peer(k) + lax.rem(c + d, 2)
                copy(cbuf.at[me], cbuf.at[s], c_send.at[0], c_recv.at[s], sibling).wait_recv()
    curve = jnp.sum(cbuf[...], axis=0)
    curve = jnp.sum(jnp.where(lane == row, curve, 0.0), axis=1, keepdims=True)
    step = norm_one / curve
    w_ref[...] = pick(alpha * own_targets + step * own_direction)
    res_ref[...] = pick(own_residual - step * image)
    for one in sends:
        one.wait_send()


def per_device(rows, embeddings, noise, targets):
    per, width = embeddings.shape
    count = targets.shape[0]
    f32, bf16 = jnp.float32, jnp.bfloat16
    dma = pltpu.SemaphoreType.DMA
    vmem = pl.BlockSpec(memory_space=pltpu.VMEM)
    return pl.pallas_call(
        functools.partial(body, rows),
        out_shape=[jax.ShapeDtypeStruct((count, per), f32)] * 2,
        in_specs=[vmem] * 3,
        out_specs=[vmem] * 2,
        scratch_shapes=[
            pltpu.VMEM((rows, per, width), bf16),
            pltpu.VMEM((2 * per, width), bf16),
            pltpu.VMEM((count, per), f32),
            pltpu.VMEM((rows, count, 2 * per), f32),
            pltpu.VMEM((rows * per, 2 * per), bf16),
            pltpu.VMEM((rows * per, 2 * per), bf16),
            pltpu.VMEM((2, count, 2 * per), f32),
            pltpu.VMEM((2, count, 2 * per), f32),
            pltpu.VMEM((rows, count, 2 * per), f32),
            pltpu.VMEM((count, rows * per), f32),
            pltpu.VMEM((2 * rows, 1, 2 * per), f32),
            dma((rows,)), dma((rows,)), dma, dma, dma, dma, dma((rows,)), dma((rows,)),
            dma((2,)), dma((2,)), dma((rows,)), dma((rows,)), dma((2 * rows,)), dma((2 * rows,)),
        ],
        compiler_params=pltpu.CompilerParams(
            collective_id=0, has_side_effects=True, vmem_limit_bytes=40 * 2**20
        ),
    )(embeddings, noise.reshape(1, per), targets)


def solution(mesh):
    in_specs = (
        P(("groups", "col", "row"), None),
        P(("groups", "col", "row")),
        P(None, ("groups", "col", "row")),
    )
    out_specs = (P(None, ("groups", "col", "row")), P(None, ("groups", "col", "row")))
    return jax.shard_map(
        functools.partial(per_device, mesh.shape["row"]),
        mesh=mesh, in_specs=in_specs, out_specs=out_specs, check_vma=False,
    )
```

```python
import functools
import math

import jax
import jax.numpy as jnp
from jax import lax
from jax.experimental import pallas as pl
from jax.experimental.pallas import tpu as pltpu
from jax.sharding import PartitionSpec as P

LAYERS = 5
MESH = pl.DeviceIdType.MESH
ARCCOS = (
    1.5707963050,
    -0.2145988016,
    0.0889789874,
    -0.0501743046,
    0.0308918810,
    -0.0170881256,
    0.0066700901,
    -0.0012624911,
)


def each(start, stop, step):
    if stop - start <= 16:
        for k in range(start, stop):
            step(k)
    else:
        lax.fori_loop(start, stop, lambda k, _: (step(k), 0)[1], 0)


def root(x):
    return x * lax.rsqrt(jnp.maximum(x, 1e-30))


def arccos_over_pi(x, root_one_minus):
    total = jnp.full_like(x, ARCCOS[-1] / math.pi)
    for coefficient in ARCCOS[-2::-1]:
        total = total * x + coefficient / math.pi
    return total * root_one_minus


def layers(first):
    rho = jnp.clip(first, -1.0, 1.0)
    kernel = first
    for layer in range(LAYERS - 1):
        size = jnp.abs(rho) if layer == 0 else rho
        rest = 1.0 - size
        angle = arccos_over_pi(size, root(rest))
        share = 1.0 - angle
        if layer == 0:
            share = jnp.where(rho < 0.0, angle, share)
        sigma = root(rest * (1.0 + size)) * (1.0 / math.pi) + share * rho
        kernel = sigma + kernel * share
        rho = jnp.minimum(sigma, 1.0)
    return kernel


def body(
    rows, e_ref, noise_hbm, t_hbm, w_ref, res_ref,
    noise_ref, t_ref, in_sem, ecol, erow, tsib, tall, khi, klo, part, psib, fall, vbuf, cbuf,
    e_send, e_recv, es_send, es_recv, ts_send, ts_recv, t_send, t_recv,
    p_send, p_recv, f_send, f_recv, c_send, c_recv,
):
    f32, bf16 = jnp.float32, jnp.bfloat16
    g, r, c = lax.axis_index("groups"), lax.axis_index("row"), lax.axis_index("col")
    per, width = e_ref.shape
    count = t_ref.shape[0]
    other = 1 - c
    sibling = (g, r, other)
    half = rows // 2
    partner = r + 1 - 2 * lax.rem(r, 2)

    def copy(src, dst, send, recv, device):
        return pltpu.make_async_remote_copy(
            src_ref=src, dst_ref=dst, send_sem=send, recv_sem=recv, device_id=device, device_id_type=MESH
        )

    def row_peer(k):
        return lax.rem(r + k, rows)

    mine = pl.ds(pl.multiple_of(c * per, per), per)
    loads = [
        pltpu.make_async_copy(t_hbm, t_ref, in_sem.at[0]),
        pltpu.make_async_copy(noise_hbm, noise_ref, in_sem.at[1]),
        pltpu.make_async_copy(e_ref, ecol.at[r], in_sem.at[2]),
        pltpu.make_async_copy(e_ref, erow.at[mine], in_sem.at[3]),
    ]
    for load in loads:
        load.start()

    barrier = pltpu.get_barrier_semaphore()

    def everyone(step):
        def one(j):
            step(row_peer(j // 2), lax.rem(c + j % 2, 2), j)

        each(1, 2 * rows, one)

    everyone(
        lambda s, d, j: pl.semaphore_signal(barrier, inc=1, device_id=(g, s, d), device_id_type=MESH)
    )
    pl.semaphore_wait(barrier, 2 * rows - 1)

    def e_direct(k):
        return copy(e_ref, ecol.at[r], e_send.at[k], e_recv.at[r], (g, row_peer(2 * k), c))

    def e_relay(k):
        s = row_peer(rows - 2 * k)
        return copy(ecol.at[s], ecol.at[s], e_send.at[half + k], e_recv.at[s], (g, partner, c))

    def t_send_to(k):
        return copy(tall.at[r], tall.at[r], t_send.at[k], t_recv.at[r], (g, row_peer(k), c))

    def f_send_to(k):
        return copy(fall.at[r], fall.at[r], f_send.at[k], f_recv.at[r], (g, row_peer(k), c))

    e_sibling = copy(e_ref, erow.at[mine], es_send, es_recv, sibling)
    e_partner = copy(e_ref, ecol.at[r], e_send.at[0], e_recv.at[r], (g, partner, c))
    t_sibling = copy(t_ref, tsib, ts_send, ts_recv, sibling)
    e_sibling.start()
    each(1, half, lambda k: e_direct(k).start())
    e_partner.start()
    loads[0].wait()
    t_sibling.start()
    first = c == 0
    lane = lax.broadcasted_iota(jnp.int32, (count, 2 * per), 1)
    row = lax.broadcasted_iota(jnp.int32, (count, 2 * per), 0)

    def pick(x):
        return jnp.where(first, x[:, :per], x[:, per:])

    t_sibling.wait_recv()
    t_mine, t_other = t_ref[...], tsib[...]
    tall[r] = jnp.where(
        first, jnp.concatenate([t_mine, t_other], axis=1), jnp.concatenate([t_other, t_mine], axis=1)
    )
    each(1, rows, lambda k: t_send_to(k).start())
    for load in loads[1:]:
        load.wait()
    noise = noise_ref[...]
    empty = jnp.zeros_like(noise)
    noise = jnp.where(
        first, jnp.concatenate([noise, empty], axis=1), jnp.concatenate([empty, noise], axis=1)
    )

    e_sibling.wait_recv()
    dims = (((1,), (1,)), ((), ()))
    block = erow[...]
    square = lax.dot_general(block, block, dims, preferred_element_type=f32)
    at = lax.broadcasted_iota(jnp.int32, square.shape, 0) == lax.broadcasted_iota(jnp.int32, square.shape, 1)
    row_norms = jnp.sum(jnp.where(at, square, 0.0), axis=0, keepdims=True) / width + 1e-05
    row_inverse = lax.rsqrt(row_norms)
    row_scale = row_norms * row_inverse / LAYERS
    row_inverse = row_inverse / width

    def gram(s):
        piece = ecol[s]
        sigma = lax.dot_general(piece, erow[...], dims, preferred_element_type=f32)
        wide = piece.astype(f32)
        norms = jnp.sum(wide * wide, axis=1, keepdims=True) / width + 1e-05
        inverse = lax.rsqrt(norms)
        kernel = layers(sigma * inverse * row_inverse)
        kernel = kernel * (norms * inverse) * row_scale
        high = kernel.astype(bf16)
        place = pl.ds(pl.multiple_of(s * per, per), per)
        khi[place, :] = high
        klo[place, :] = (kernel - high.astype(f32)).astype(bf16)

    def arrived(s):
        copy(e_ref, ecol.at[s], e_send.at[0], e_recv.at[s], (g, partner, c)).wait_recv()

    gram(r)
    arrived(partner)
    gram(partner)

    def same_side(k):
        s = row_peer(rows - 2 * k)
        arrived(s)
        e_relay(k).start()
        gram(s)

    def far_side(k):
        s = lax.rem(partner + rows - 2 * k, rows)
        arrived(s)
        gram(s)

    each(1, half, same_side)
    each(1, half, far_side)

    def t_arrived(k):
        s = row_peer(k)
        copy(tall.at[r], tall.at[s], t_send.at[k], t_recv.at[s], (g, s, c)).wait_recv()

    each(1, rows, t_arrived)

    def columns(vector):
        for k in range(half):
            a, b = vector[2 * k], vector[2 * k + 1]
            a = jnp.where(first, a, pltpu.roll(a, per, 1))
            b = jnp.where(first, pltpu.roll(b, per, 1), b)
            vbuf[:, 2 * per * k : 2 * per * (k + 1)] = jnp.where(lane < per, a, b)

    def apply(own):
        v = vbuf[...]
        high = v.astype(bf16)
        low = (v - high.astype(f32)).astype(bf16)
        both = jnp.concatenate([high, low], axis=0)
        a = jnp.dot(both, khi[...], preferred_element_type=f32)
        b = jnp.dot(high, klo[...], preferred_element_type=f32)
        return a[:count] + a[count:] + b + noise * own

    def total(x):
        return jnp.sum(jnp.sum(x, axis=0), axis=1, keepdims=True)

    targets = tall[...]
    columns(targets)
    own_targets = tall[r]
    mine_part = apply(own_targets)
    part[0] = mine_part
    p_one = copy(part.at[0], psib.at[0], p_send.at[0], p_recv.at[0], sibling)
    p_one.start()
    p_one.wait_recv()
    fall[r] = mine_part + psib[0]
    each(1, rows, lambda k: f_send_to(k).start())
    norm_zero = total(targets * targets)

    def f_arrived(k):
        s = row_peer(k)
        copy(fall.at[r], fall.at[s], f_send.at[k], f_recv.at[s], (g, s, c)).wait_recv()

    each(1, rows, f_arrived)
    image = fall[...]
    alpha = norm_zero / total(targets * image)
    residual = targets - alpha[None] * image
    norm_one = total(residual * residual)
    beta = norm_one / norm_zero

    columns(residual + beta[None] * targets)
    own_residual = own_targets - alpha * fall[r]
    own_direction = own_residual + beta * own_targets
    mine_part = apply(own_direction)
    part[1] = mine_part
    p_two = copy(part.at[1], psib.at[1], p_send.at[1], p_recv.at[1], sibling)
    p_two.start()
    curve = jnp.sum(own_direction * mine_part, axis=1, keepdims=True)
    me = 2 * r + c
    cbuf[me] = jnp.sum(jnp.where(lane == row, curve, 0.0), axis=0, keepdims=True)

    def c_send_to(s, d, j):
        return copy(cbuf.at[me], cbuf.at[me], c_send.at[j], c_recv.at[me], (g, s, d))

    everyone(lambda s, d, j: c_send_to(s, d, j).start())
    p_two.wait_recv()
    image = mine_part + psib[1]
    everyone(
        lambda s, d, j: copy(
            cbuf.at[me], cbuf.at[2 * s + d], c_send.at[j], c_recv.at[2 * s + d], (g, s, d)
        ).wait_recv()
    )
    curve = jnp.sum(cbuf[...], axis=0)
    curve = jnp.sum(jnp.where(lane == row, curve, 0.0), axis=1, keepdims=True)
    step = norm_one / curve
    w_ref[...] = pick(alpha * own_targets + step * own_direction)
    res_ref[...] = pick(own_residual - step * image)
    for one in (e_sibling, e_partner, t_sibling, p_one, p_two):
        one.wait_send()

    def sent(k):
        t_send_to(k).wait_send()
        f_send_to(k).wait_send()

    def e_sent(k):
        e_direct(k).wait_send()
        e_relay(k).wait_send()

    each(1, half, e_sent)
    each(1, rows, sent)
    everyone(lambda s, d, j: c_send_to(s, d, j).wait_send())


def per_device(rows, embeddings, noise, targets):
    per, width = embeddings.shape
    count = targets.shape[0]
    f32, bf16 = jnp.float32, jnp.bfloat16
    dma = pltpu.SemaphoreType.DMA
    vmem = pl.BlockSpec(memory_space=pltpu.VMEM)
    return pl.pallas_call(
        functools.partial(body, rows),
        out_shape=[jax.ShapeDtypeStruct((count, per), f32)] * 2,
        in_specs=[pl.BlockSpec(memory_space=pltpu.HBM)] * 3,
        out_specs=[vmem] * 2,
        scratch_shapes=[
            pltpu.VMEM((1, per), f32),
            pltpu.VMEM((count, per), f32),
            dma((4,)),
            pltpu.VMEM((rows, per, width), bf16),
            pltpu.VMEM((2 * per, width), bf16),
            pltpu.VMEM((count, per), f32),
            pltpu.VMEM((rows, count, 2 * per), f32),
            pltpu.VMEM((rows * per, 2 * per), bf16),
            pltpu.VMEM((rows * per, 2 * per), bf16),
            pltpu.VMEM((2, count, 2 * per), f32),
            pltpu.VMEM((2, count, 2 * per), f32),
            pltpu.VMEM((rows, count, 2 * per), f32),
            pltpu.VMEM((count, rows * per), f32),
            pltpu.VMEM((2 * rows, 1, 2 * per), f32),
            dma((rows,)), dma((rows,)), dma, dma, dma, dma, dma((rows,)), dma((rows,)),
            dma((2,)), dma((2,)), dma((rows,)), dma((rows,)), dma((2 * rows,)), dma((2 * rows,)),
        ],
        compiler_params=pltpu.CompilerParams(
            collective_id=0, has_side_effects=True, vmem_limit_bytes=40 * 2**20
        ),
    )(embeddings, noise.reshape(1, per), targets)


def solution(mesh):
    in_specs = (
        P(("groups", "col", "row"), None),
        P(("groups", "col", "row")),
        P(None, ("groups", "col", "row")),
    )
    out_specs = (P(None, ("groups", "col", "row")), P(None, ("groups", "col", "row")))
    return jax.shard_map(
        functools.partial(per_device, mesh.shape["row"]),
        mesh=mesh, in_specs=in_specs, out_specs=out_specs, check_vma=False,
    )
```

```python
import functools
import math

import jax
import jax.numpy as jnp
from jax import lax
from jax.experimental import pallas as pl
from jax.experimental.pallas import tpu as pltpu
from jax.sharding import PartitionSpec as P

LAYERS = 5
MESH = pl.DeviceIdType.MESH
ARCCOS = (
    1.5707963050,
    -0.2145988016,
    0.0889789874,
    -0.0501743046,
    0.0308918810,
    -0.0170881256,
    0.0066700901,
    -0.0012624911,
)


def each(start, stop, step):
    if stop - start <= 16:
        for k in range(start, stop):
            step(k)
    else:
        lax.fori_loop(start, stop, lambda k, _: (step(k), 0)[1], 0)


def root(x):
    return x * lax.rsqrt(jnp.maximum(x, 1e-30))


def arccos_over_pi(x, root_one_minus):
    total = jnp.full_like(x, ARCCOS[-1] / math.pi)
    for coefficient in ARCCOS[-2::-1]:
        total = total * x + coefficient / math.pi
    return total * root_one_minus


def layers(first):
    rho = jnp.clip(first, -1.0, 1.0)
    kernel = first
    for layer in range(LAYERS - 1):
        size = jnp.abs(rho) if layer == 0 else rho
        rest = 1.0 - size
        angle = arccos_over_pi(size, root(rest))
        share = 1.0 - angle
        if layer == 0:
            share = jnp.where(rho < 0.0, angle, share)
        sigma = root(rest * (1.0 + size)) * (1.0 / math.pi) + share * rho
        kernel = sigma + kernel * share
        rho = jnp.minimum(sigma, 1.0)
    return kernel


def body(
    rows, e_ref, noise_hbm, t_hbm, w_ref, res_ref,
    noise_ref, t_ref, in_sem, line, plane, tpart, tall, khi, klo, parts, fall, dall, vbuf, pick, cbuf,
    e_send, e_recv, b_send, b_recv, tp_send, tp_recv, t_send, t_recv,
    p_send, p_recv, f_send, f_recv, c_send, c_recv,
):
    f32, bf16 = jnp.float32, jnp.bfloat16
    g, r, c = lax.axis_index("groups"), lax.axis_index("row"), lax.axis_index("col")
    per, width = e_ref.shape
    count = t_ref.shape[0]
    depth = rows // 2
    z, x = r // 2, lax.rem(r, 2)
    q = 2 * x + c
    wide = 4 * per

    def copy(src, dst, send, recv, device):
        return pltpu.make_async_remote_copy(
            src_ref=src, dst_ref=dst, send_sem=send, recv_sem=recv, device_id=device, device_id_type=MESH
        )

    def at_plane(k):
        p = lax.rem(q + k, 4)
        return p, (g, 2 * z + p // 2, lax.rem(p, 2))

    def at_line(k):
        s = lax.rem(z + k, depth)
        return s, (g, 2 * s + x, c)

    def place(p):
        return pl.ds(pl.multiple_of(p * per, per), per)

    loads = [
        pltpu.make_async_copy(t_hbm, t_ref, in_sem.at[0]),
        pltpu.make_async_copy(noise_hbm, noise_ref, in_sem.at[1]),
        pltpu.make_async_copy(e_ref, line.at[z], in_sem.at[2]),
        pltpu.make_async_copy(e_ref, plane.at[place(q)], in_sem.at[3]),
    ]
    for load in loads:
        load.start()

    barrier = pltpu.get_barrier_semaphore()

    def greet(device):
        pl.semaphore_signal(barrier, inc=1, device_id=device, device_id_type=MESH)

    each(1, depth, lambda k: greet(at_line(k)[1]))
    each(1, 4, lambda k: greet(at_plane(k)[1]))
    pl.semaphore_wait(barrier, depth + 2)

    def e_line(k):
        return copy(e_ref, line.at[z], e_send.at[k], e_recv.at[z], at_line(k)[1])

    def e_plane(k):
        return copy(e_ref, plane.at[place(q)], b_send.at[k], b_recv.at[q], at_plane(k)[1])

    def t_plane(k):
        return copy(t_ref, tpart.at[q], tp_send.at[k], tp_recv.at[q], at_plane(k)[1])

    def t_line(k):
        return copy(tall.at[z], tall.at[z], t_send.at[k], t_recv.at[z], at_line(k)[1])

    def p_plane(i, k):
        return copy(
            parts.at[i, q], parts.at[i, q], p_send.at[i, k], p_recv.at[i, q], at_plane(k)[1]
        )

    def f_line(k):
        return copy(fall.at[z], fall.at[z], f_send.at[k], f_recv.at[z], at_line(k)[1])

    each(1, depth, lambda k: e_line(k).start())
    each(1, 4, lambda k: e_plane(k).start())
    loads[0].wait()
    each(1, 4, lambda k: t_plane(k).start())
    for load in loads[1:]:
        load.wait()
    tpart[q] = t_ref[...]

    first = c == 0
    lane = lax.broadcasted_iota(jnp.int32, (count, 2 * per), 1)
    row = lax.broadcasted_iota(jnp.int32, (count, 2 * per), 0)
    spot = lax.broadcasted_iota(jnp.int32, (1, wide), 1) // per
    noise = noise_ref[...]
    noise = jnp.where(spot == q, jnp.concatenate([noise] * 4, axis=1), 0.0)

    def from_plane(k, source, target, send, recv):
        p, device = at_plane(k)
        copy(source, target(p), send.at[k], recv.at[p], device).wait_recv()

    def from_line(k, target, send, recv):
        s, device = at_line(k)
        copy(target.at[s], target.at[s], send.at[k], recv.at[s], device).wait_recv()

    each(1, 4, lambda k: from_plane(k, t_ref, lambda p: tpart.at[p], tp_send, tp_recv))
    tall[z] = jnp.concatenate([tpart[p] for p in range(4)], axis=1)
    each(1, depth, lambda k: t_line(k).start())

    each(1, 4, lambda k: from_plane(k, e_ref, lambda p: plane.at[place(p)], b_send, b_recv))
    dims = (((1,), (1,)), ((), ()))
    block = plane[...]
    square = lax.dot_general(block, block, dims, preferred_element_type=f32)
    at = lax.broadcasted_iota(jnp.int32, square.shape, 0) == lax.broadcasted_iota(jnp.int32, square.shape, 1)
    row_norms = jnp.sum(jnp.where(at, square, 0.0), axis=0, keepdims=True) / width + 1e-05
    row_inverse = lax.rsqrt(row_norms)
    row_scale = row_norms * row_inverse / LAYERS
    row_inverse = row_inverse / width

    def gram(s):
        piece = line[s]
        sigma = lax.dot_general(piece, plane[...], dims, preferred_element_type=f32)
        values = piece.astype(f32)
        norms = jnp.sum(values * values, axis=1, keepdims=True) / width + 1e-05
        inverse = lax.rsqrt(norms)
        kernel = layers(sigma * inverse * row_inverse)
        kernel = kernel * (norms * inverse) * row_scale
        high = kernel.astype(bf16)
        khi[place(s), :] = high
        klo[place(s), :] = (kernel - high.astype(f32)).astype(bf16)

    gram(z)

    def arrived(k):
        from_line(k, line, e_send, e_recv)
        gram(at_line(k)[0])

    each(1, depth, arrived)
    each(1, depth, lambda k: from_line(k, tall, t_send, t_recv))

    def columns(vector):
        side = pl.ds(pl.multiple_of(x * 2 * per, 2 * per), 2 * per)
        for k in range(depth // 2):
            a, b = vector[2 * k, :, side], vector[2 * k + 1, :, side]
            a = jnp.where(first, a, pltpu.roll(a, per, 1))
            b = jnp.where(first, pltpu.roll(b, per, 1), b)
            vbuf[:, 2 * per * k : 2 * per * (k + 1)] = jnp.where(lane < per, a, b)

    def apply(own):
        v = vbuf[...]
        high = v.astype(bf16)
        low = (v - high.astype(f32)).astype(bf16)
        both = jnp.concatenate([high, low], axis=0)
        a = jnp.dot(both, khi[...], preferred_element_type=f32)
        b = jnp.dot(high, klo[...], preferred_element_type=f32)
        return a[:count] + a[count:] + b + noise * own

    def total(values):
        return jnp.sum(jnp.sum(values, axis=0), axis=1, keepdims=True)

    def summed(i):
        each(1, 4, lambda k: from_plane(k, parts.at[i, q], lambda p: parts.at[i, p], p_send.at[i], p_recv.at[i]))
        return (parts[i, 0] + parts[i, 1]) + (parts[i, 2] + parts[i, 3])

    columns(tall)
    own_targets = tall[z]
    parts[0, q] = apply(own_targets)
    each(1, 4, lambda k: p_plane(0, k).start())
    targets = tall[...]
    norm_zero = total(targets * targets)
    own_image = summed(0)
    fall[z] = own_image
    each(1, depth, lambda k: f_line(k).start())
    each(1, depth, lambda k: from_line(k, fall, f_send, f_recv))
    image = fall[...]
    alpha = norm_zero / total(targets * image)
    residual = targets - alpha[None] * image
    norm_one = total(residual * residual)
    beta = norm_one / norm_zero

    dall[...] = residual + beta[None] * targets
    columns(dall)
    own_residual = own_targets - alpha * own_image
    own_direction = own_residual + beta * own_targets
    mine = apply(own_direction)
    curve = jnp.sum(own_direction * mine, axis=1, keepdims=True)
    me = 2 * r + c
    cbuf[me] = jnp.sum(jnp.where(lane == row, curve, 0.0), axis=0, keepdims=True)

    def everyone(step):
        def one(j):
            step(lax.rem(r + j // 2, rows), lax.rem(c + j % 2, 2), j)

        each(1, 2 * rows, one)

    def c_send_to(s, d, j):
        return copy(cbuf.at[me], cbuf.at[me], c_send.at[j], c_recv.at[me], (g, s, d))

    everyone(lambda s, d, j: c_send_to(s, d, j).start())
    parts[1, q] = mine
    each(1, 4, lambda k: p_plane(1, k).start())
    own_image = summed(1)
    everyone(
        lambda s, d, j: copy(
            cbuf.at[me], cbuf.at[2 * s + d], c_send.at[j], c_recv.at[2 * s + d], (g, s, d)
        ).wait_recv()
    )
    curve = jnp.sum(cbuf[...], axis=0)
    curve = jnp.sum(jnp.where(lane == row, curve, 0.0), axis=1, keepdims=True)
    step = norm_one / curve

    def own(values):
        pick[...] = values
        part = pick[:, pl.ds(pl.multiple_of(x * 2 * per, 2 * per), 2 * per)]
        return jnp.where(first, part[:, :per], part[:, per:])

    w_ref[...] = own(alpha * own_targets + step * own_direction)
    res_ref[...] = own(own_residual - step * own_image)

    def plane_sent(k):
        for one in (e_plane(k), t_plane(k), p_plane(0, k), p_plane(1, k)):
            one.wait_send()

    def line_sent(k):
        for one in (e_line(k), t_line(k), f_line(k)):
            one.wait_send()

    each(1, 4, plane_sent)
    each(1, depth, line_sent)
    everyone(lambda s, d, j: c_send_to(s, d, j).wait_send())


def per_device(rows, embeddings, noise, targets):
    per, width = embeddings.shape
    count = targets.shape[0]
    depth, wide = rows // 2, 4 * per
    f32, bf16 = jnp.float32, jnp.bfloat16
    dma = pltpu.SemaphoreType.DMA
    vmem = pl.BlockSpec(memory_space=pltpu.VMEM)
    return pl.pallas_call(
        functools.partial(body, rows),
        out_shape=[jax.ShapeDtypeStruct((count, per), f32)] * 2,
        in_specs=[pl.BlockSpec(memory_space=pltpu.HBM)] * 3,
        out_specs=[vmem] * 2,
        scratch_shapes=[
            pltpu.VMEM((1, per), f32),
            pltpu.VMEM((count, per), f32),
            dma((4,)),
            pltpu.VMEM((depth, per, width), bf16),
            pltpu.VMEM((wide, width), bf16),
            pltpu.VMEM((4, count, per), f32),
            pltpu.VMEM((depth, count, wide), f32),
            pltpu.VMEM((depth * per, wide), bf16),
            pltpu.VMEM((depth * per, wide), bf16),
            pltpu.VMEM((2, 4, count, wide), f32),
            pltpu.VMEM((depth, count, wide), f32),
            pltpu.VMEM((depth, count, wide), f32),
            pltpu.VMEM((count, depth * per), f32),
            pltpu.VMEM((count, wide), f32),
            pltpu.VMEM((2 * rows, 1, 2 * per), f32),
            dma((depth,)), dma((depth,)), dma((4,)), dma((4,)), dma((4,)), dma((4,)),
            dma((depth,)), dma((depth,)), dma((2, 4)), dma((2, 4)),
            dma((depth,)), dma((depth,)), dma((2 * rows,)), dma((2 * rows,)),
        ],
        compiler_params=pltpu.CompilerParams(
            collective_id=0, has_side_effects=True, vmem_limit_bytes=60 * 2**20
        ),
    )(embeddings, noise.reshape(1, per), targets)


def solution(mesh):
    in_specs = (
        P(("groups", "col", "row"), None),
        P(("groups", "col", "row")),
        P(None, ("groups", "col", "row")),
    )
    out_specs = (P(None, ("groups", "col", "row")), P(None, ("groups", "col", "row")))
    return jax.shard_map(
        functools.partial(per_device, mesh.shape["row"]),
        mesh=mesh, in_specs=in_specs, out_specs=out_specs, check_vma=False,
    )
```

```python
import functools
import math

import jax
import jax.numpy as jnp
from jax import lax
from jax.experimental import pallas as pl
from jax.experimental.pallas import tpu as pltpu
from jax.sharding import PartitionSpec as P

LAYERS = 5
MESH = pl.DeviceIdType.MESH
ARCCOS = (
    1.5707963050,
    -0.2145988016,
    0.0889789874,
    -0.0501743046,
    0.0308918810,
    -0.0170881256,
    0.0066700901,
    -0.0012624911,
)


def each(start, stop, step):
    if stop - start <= 16:
        for k in range(start, stop):
            step(k)
    else:
        lax.fori_loop(start, stop, lambda k, _: (step(k), 0)[1], 0)


def peer(me, k, count):
    if count & (count - 1):
        return lax.rem(me + k, count)
    found, bit = 0, 1
    while bit < count:
        mine, turn = lax.rem(me // bit, 2), (k // bit) % 2
        found, bit = found + bit * (mine + turn - 2 * mine * turn), 2 * bit
    return found


def root(x):
    return x * lax.rsqrt(jnp.maximum(x, 1e-30))


def arccos_over_pi(x, root_one_minus):
    total = jnp.full_like(x, ARCCOS[-1] / math.pi)
    for coefficient in ARCCOS[-2::-1]:
        total = total * x + coefficient / math.pi
    return total * root_one_minus


def layers(first):
    rho = jnp.clip(first, -1.0, 1.0)
    kernel = first
    for layer in range(LAYERS - 1):
        size = jnp.abs(rho) if layer == 0 else rho
        rest = 1.0 - size
        angle = arccos_over_pi(size, root(rest))
        share = 1.0 - angle
        if layer == 0:
            share = jnp.where(rho < 0.0, angle, share)
        sigma = root(rest * (1.0 + size)) * (1.0 / math.pi) + share * rho
        kernel = sigma + kernel * share
        rho = jnp.minimum(sigma, 1.0)
    return kernel


def body(
    rows, e_ref, noise_hbm, t_hbm, out_ref,
    noise_ref, t_ref, in_sem, line, plane, tsib, tline, khi, klo, part, psib, fall, dall, rest, pown, vbuf, cbuf,
    e_send, e_recv, b_send, b_recv, s_send, s_recv, t_send, t_recv,
    p_send, p_recv, f_send, f_recv, c_send, c_recv,
):
    f32, bf16 = jnp.float32, jnp.bfloat16
    g, r, c = lax.axis_index("groups"), lax.axis_index("row"), lax.axis_index("col")
    per, width = e_ref.shape
    count = t_ref.shape[0]
    some = count // 2
    depth = rows // 2
    z, x = r // 2, lax.rem(r, 2)
    q = 2 * x + c
    pair, wide = 2 * per, 4 * per
    other = 1 - c
    sibling = (g, r, other)

    def copy(src, dst, send, recv, device):
        return pltpu.make_async_remote_copy(
            src_ref=src, dst_ref=dst, send_sem=send, recv_sem=recv, device_id=device, device_id_type=MESH
        )

    def at_plane(k):
        p = peer(q, k, 4)
        return p, (g, 2 * z + p // 2, lax.rem(p, 2))

    def at_line(k):
        s = peer(z, k, depth)
        return s, (g, 2 * s + x, c)

    def at_row(k):
        s = peer(r, k, rows)
        return s, (g, s, c)

    def place(p):
        return pl.ds(pl.multiple_of(p * per, per), per)

    def side(p):
        return pl.ds(pl.multiple_of(p * pair, pair), pair)

    def share(d):
        return pl.ds(pl.multiple_of(d * some, some), some)

    loads = [
        pltpu.make_async_copy(t_hbm, t_ref, in_sem.at[0]),
        pltpu.make_async_copy(noise_hbm, noise_ref, in_sem.at[1]),
        pltpu.make_async_copy(e_ref, line.at[z], in_sem.at[2]),
        pltpu.make_async_copy(e_ref, plane.at[place(q)], in_sem.at[3]),
        pltpu.make_async_copy(t_hbm, tline.at[z], in_sem.at[4]),
    ]
    for load in loads:
        load.start()

    barrier = pltpu.get_barrier_semaphore()

    def greet(device):
        pl.semaphore_signal(barrier, inc=1, device_id=device, device_id_type=MESH)

    each(1, depth, lambda k: greet(at_line(k)[1]))
    each(1, 4, lambda k: greet(at_plane(k)[1]))
    pl.semaphore_wait(barrier, depth + 2)

    def e_line(k):
        return copy(e_ref, line.at[z], e_send.at[k], e_recv.at[z], at_line(k)[1])

    def e_plane(k):
        return copy(e_ref, plane.at[place(q)], b_send.at[k], b_recv.at[q], at_plane(k)[1])

    def t_row(k):
        return copy(t_hbm, tline.at[z], t_send.at[k], t_recv.at[z], at_line(k)[1])

    def t_from(k):
        s, device = at_line(k)
        return copy(t_hbm, tline.at[s], t_send.at[k], t_recv.at[s], device)

    def f_row(k):
        return copy(fall.at[r], fall.at[r], f_send.at[k], f_recv.at[r], at_row(k)[1])

    def f_from(k):
        s = at_row(k)[0]
        return copy(fall.at[s], fall.at[s], f_send.at[k], f_recv.at[s], at_row(k)[1])

    def p_plane(k):
        p, device = at_plane(k)
        return copy(part.at[1, :, side(p // 2)], pown.at[q], p_send.at[k], p_recv.at[q], device)

    def p_from(k):
        p, device = at_plane(k)
        return copy(pown.at[p], pown.at[p], p_send.at[k], p_recv.at[p], device)

    def between(i, src, dst):
        return copy(src, dst, s_send.at[i], s_recv.at[i], sibling)

    t_first = between(0, t_ref.at[share(other)], tsib)
    p_first = between(1, part.at[0, share(other)], psib)
    d_first = between(2, dall.at[c], dall.at[c])
    d_rest = between(3, rest.at[c], rest.at[c])

    each(1, depth, lambda k: e_line(depth - k).start())
    each(1, depth, lambda k: t_row(depth - k).start())
    each(1, 4, lambda k: e_plane(4 - k).start())
    loads[0].wait()
    t_first.start()

    first = c == 0
    lane = lax.broadcasted_iota(jnp.int32, (count, pair), 1)
    row = lax.broadcasted_iota(jnp.int32, (count, pair), 0)
    spot = lax.broadcasted_iota(jnp.int32, (1, wide), 1) // per

    for load in loads[1:]:
        load.wait()
    noise = noise_ref[...]
    noise = jnp.where(spot == q, jnp.concatenate([noise] * 4, axis=1), 0.0)

    def b_arrived(k):
        p, device = at_plane(k)
        copy(e_ref, plane.at[place(p)], b_send.at[k], b_recv.at[p], device).wait_recv()

    each(1, 4, b_arrived)
    dims = (((1,), (1,)), ((), ()))
    block = plane[...]
    square = lax.dot_general(block, block, dims, preferred_element_type=f32)
    at = lax.broadcasted_iota(jnp.int32, square.shape, 0) == lax.broadcasted_iota(jnp.int32, square.shape, 1)
    row_norms = jnp.sum(jnp.where(at, square, 0.0), axis=0, keepdims=True) / width + 1e-05
    row_inverse = lax.rsqrt(row_norms)
    row_scale = row_norms * row_inverse / LAYERS
    row_inverse = row_inverse / width

    def gram(s):
        piece = line[s]
        sigma = lax.dot_general(piece, plane[...], dims, preferred_element_type=f32)
        values = piece.astype(f32)
        norms = jnp.sum(values * values, axis=1, keepdims=True) / width + 1e-05
        inverse = lax.rsqrt(norms)
        kernel = layers(sigma * inverse * row_inverse)
        kernel = kernel * (norms * inverse) * row_scale
        high = kernel.astype(bf16)
        khi[place(s), :] = high
        klo[place(s), :] = (kernel - high.astype(f32)).astype(bf16)

    gram(z)
    t_mine = t_ref[share(c), :]
    t_first.wait_recv()
    t_other = tsib[...]
    fall[r, :, wide:] = jnp.where(
        first, jnp.concatenate([t_mine, t_other], axis=1), jnp.concatenate([t_other, t_mine], axis=1)
    )
    each(1, depth, lambda k: t_from(k).wait_recv())
    vbuf[...] = jnp.concatenate([tline[k] for k in range(depth)], axis=1)

    def arrived(k):
        s, device = at_line(k)
        copy(e_ref, line.at[s], e_send.at[k], e_recv.at[s], device).wait_recv()
        gram(s)

    each(1, depth, arrived)

    def whole(ref, s, lanes):
        return jnp.concatenate([ref[0, s, :, lanes], ref[1, s, :, lanes]], axis=0)

    def columns(ref):
        for k in range(depth // 2):
            a, b = whole(ref, 2 * k, side(x)), whole(ref, 2 * k + 1, side(x))
            a = jnp.where(first, a, pltpu.roll(a, per, 1))
            b = jnp.where(first, pltpu.roll(b, per, 1), b)
            vbuf[:, pair * k : pair * (k + 1)] = jnp.where(lane < per, a, b)

    def apply(own):
        v = vbuf[...]
        high = v.astype(bf16)
        low = (v - high.astype(f32)).astype(bf16)
        both = jnp.concatenate([high, low], axis=0)
        a = jnp.dot(both, khi[...], preferred_element_type=f32)
        b = jnp.dot(high, klo[...], preferred_element_type=f32)
        return a[:count] + a[count:] + b + noise * own

    def total(values):
        return jnp.sum(jnp.sum(values, axis=0), axis=1, keepdims=True)

    own_targets = t_ref[...]
    part[0] = apply(jnp.concatenate([own_targets] * 4, axis=1))
    p_first.start()
    p_first.wait_recv()
    fall[r, :, :wide] = part[0, share(c), :] + psib[...]
    each(1, rows, lambda k: f_row(rows - k).start())
    each(1, rows, lambda k: f_from(k).wait_recv())
    held = fall[...].reshape(depth, 2, some, wide + pair)
    image = held[:, 0, :, :wide] + held[:, 1, :, :wide]
    targets = jnp.concatenate([held[:, 0, :, wide:], held[:, 1, :, wide:]], axis=2)
    norm_zero = total(targets * targets)
    alpha = norm_zero / total(targets * image)
    residual = targets - alpha[None] * image
    norm_one = total(residual * residual)
    beta = norm_one / norm_zero
    dall[c] = residual + beta[None] * targets
    d_first.start()
    even, odd = fall[2 * z], fall[2 * z + 1]
    image = even[:, :wide] + odd[:, :wide]
    rest[c, 0] = jnp.concatenate([even[:, wide:], odd[:, wide:]], axis=1) - alpha * image
    rest[c, 1] = jnp.broadcast_to(alpha, (some, wide))
    rest[c, 2] = jnp.broadcast_to(norm_one, (some, wide))
    d_rest.start()
    d_first.wait_recv()

    columns(dall)
    own_direction = whole(dall, z, slice(None))
    mine = apply(own_direction)
    curve = jnp.sum(own_direction * mine, axis=1, keepdims=True)
    me = 2 * r + c
    cbuf[me] = jnp.sum(jnp.where(lane == row, curve, 0.0), axis=0, keepdims=True)

    def everyone(step):
        def one(j):
            j = 2 * rows - j
            other_me = peer(me, j, 2 * rows)
            step(other_me // 2, lax.rem(other_me, 2), j)

        each(1, 2 * rows, one)

    def c_send_to(s, d, j):
        return copy(cbuf.at[me], cbuf.at[me], c_send.at[j], c_recv.at[me], (g, s, d))

    everyone(lambda s, d, j: c_send_to(s, d, j).start())
    part[1] = mine
    each(1, 4, lambda k: p_plane(k).start())
    pown[q] = part[1, :, side(x)]
    d_rest.wait_recv()

    def own(values):
        return jnp.where(first, values[:, :per], values[:, per:])

    def own_rest(i):
        return own(jnp.concatenate([rest[0, i, :, side(x)], rest[1, i, :, side(x)]], axis=0))

    own_residual, alpha, norm_one = own_rest(0), own_rest(1), own_rest(2)
    own_direction = own(whole(dall, z, side(x)))
    own_weights = alpha * own_targets
    each(1, 4, lambda k: p_from(k).wait_recv())
    own_image = own((pown[0] + pown[1]) + (pown[2] + pown[3]))
    everyone(
        lambda s, d, j: copy(
            cbuf.at[me], cbuf.at[2 * s + d], c_send.at[j], c_recv.at[2 * s + d], (g, s, d)
        ).wait_recv()
    )
    curve = jnp.sum(cbuf[...], axis=0)
    curve = jnp.sum(jnp.where(lane == row, curve, 0.0), axis=1, keepdims=True)
    step = norm_one / curve
    out_ref[0] = own_weights + step * own_direction
    out_ref[1] = own_residual - step * own_image

    for one in (t_first, p_first, d_first, d_rest):
        one.wait_send()

    def plane_sent(k):
        e_plane(k).wait_send()
        p_plane(k).wait_send()

    def line_sent(k):
        e_line(k).wait_send()
        t_row(k).wait_send()

    def row_sent(k):
        f_row(k).wait_send()

    each(1, 4, plane_sent)
    each(1, depth, line_sent)
    each(1, rows, row_sent)
    everyone(lambda s, d, j: c_send_to(s, d, j).wait_send())


def per_device(rows, embeddings, noise, targets):
    per, width = embeddings.shape
    count = targets.shape[0]
    some, depth, pair, wide = count // 2, rows // 2, 2 * per, 4 * per
    f32, bf16 = jnp.float32, jnp.bfloat16
    dma = pltpu.SemaphoreType.DMA
    vmem = pl.BlockSpec(memory_space=pltpu.VMEM)
    out = pl.pallas_call(
        functools.partial(body, rows),
        out_shape=jax.ShapeDtypeStruct((2, count, per), f32),
        in_specs=[pl.BlockSpec(memory_space=pltpu.HBM)] * 3,
        out_specs=vmem,
        scratch_shapes=[
            pltpu.VMEM((1, per), f32),
            pltpu.VMEM((count, per), f32),
            dma((5,)),
            pltpu.VMEM((depth, per, width), bf16),
            pltpu.VMEM((wide, width), bf16),
            pltpu.VMEM((some, per), f32),
            pltpu.VMEM((depth, count, per), f32),
            pltpu.VMEM((depth * per, wide), bf16),
            pltpu.VMEM((depth * per, wide), bf16),
            pltpu.VMEM((2, count, wide), f32),
            pltpu.VMEM((some, wide), f32),
            pltpu.VMEM((rows, some, wide + pair), f32),
            pltpu.VMEM((2, depth, some, wide), f32),
            pltpu.VMEM((2, 3, some, wide), f32),
            pltpu.VMEM((4, count, pair), f32),
            pltpu.VMEM((count, depth * per), f32),
            pltpu.VMEM((2 * rows, 1, pair), f32),
            dma((depth,)), dma((depth,)), dma((4,)), dma((4,)), dma((4,)), dma((4,)),
            dma((depth,)), dma((depth,)), dma((4,)), dma((4,)),
            dma((rows,)), dma((rows,)), dma((2 * rows,)), dma((2 * rows,)),
        ],
        compiler_params=pltpu.CompilerParams(
            collective_id=0, has_side_effects=True, vmem_limit_bytes=60 * 2**20
        ),
    )(embeddings, noise.reshape(1, per), targets)
    return out[0], out[1]


def solution(mesh):
    in_specs = (
        P(("groups", "col", "row"), None),
        P(("groups", "col", "row")),
        P(None, ("groups", "col", "row")),
    )
    out_specs = (P(None, ("groups", "col", "row")), P(None, ("groups", "col", "row")))
    return jax.shard_map(
        functools.partial(per_device, mesh.shape["row"]),
        mesh=mesh, in_specs=in_specs, out_specs=out_specs, check_vma=False,
    )
```

```python
import functools
import math

import jax
import jax.numpy as jnp
from jax import lax
from jax.experimental import pallas as pl
from jax.experimental.pallas import tpu as pltpu
from jax.sharding import PartitionSpec as P

LAYERS = 5
MESH = pl.DeviceIdType.MESH
ARCCOS = (
    1.5707963050,
    -0.2145988016,
    0.0889789874,
    -0.0501743046,
    0.0308918810,
    -0.0170881256,
    0.0066700901,
    -0.0012624911,
)


def each(start, stop, step):
    if stop - start <= 16:
        for k in range(start, stop):
            step(k)
    else:
        lax.fori_loop(start, stop, lambda k, _: (step(k), 0)[1], 0)


def peer(me, k, count):
    if count & (count - 1):
        return lax.rem(me + k, count)
    found, bit = 0, 1
    while bit < count:
        mine, turn = lax.rem(me // bit, 2), (k // bit) % 2
        found, bit = found + bit * (mine + turn - 2 * mine * turn), 2 * bit
    return found


def root(x):
    return x * lax.rsqrt(jnp.maximum(x, 1e-30))


def arccos_over_pi(x, root_one_minus):
    total = jnp.full_like(x, ARCCOS[-1] / math.pi)
    for coefficient in ARCCOS[-2::-1]:
        total = total * x + coefficient / math.pi
    return total * root_one_minus


def layers(first):
    rho = jnp.clip(first, -1.0, 1.0)
    kernel = first
    for layer in range(LAYERS - 1):
        size = jnp.abs(rho) if layer == 0 else rho
        rest = 1.0 - size
        angle = arccos_over_pi(size, root(rest))
        share = 1.0 - angle
        if layer == 0:
            share = jnp.where(rho < 0.0, angle, share)
        sigma = root(rest * (1.0 + size)) * (1.0 / math.pi) + share * rho
        kernel = sigma + kernel * share
        rho = jnp.minimum(sigma, 1.0)
    return kernel


def body(
    rows, e_ref, noise_hbm, t_hbm, out_ref,
    noise_ref, t_ref, in_sem, line, plane, tsib, tline, khi, klo, part, psib, fall, dall, rest, pown, vbuf, cbuf,
    e_send, e_recv, b_send, b_recv, s_send, s_recv, t_send, t_recv,
    p_send, p_recv, f_send, f_recv, c_send, c_recv,
):
    f32, bf16 = jnp.float32, jnp.bfloat16
    g, r, c = lax.axis_index("groups"), lax.axis_index("row"), lax.axis_index("col")
    per, width = e_ref.shape
    count = t_ref.shape[0]
    some = count // 2
    depth = rows // 2
    z, x = r // 2, lax.rem(r, 2)
    q = 2 * x + c
    pair, wide = 2 * per, 4 * per
    other = 1 - c
    sibling = (g, r, other)

    def copy(src, dst, send, recv, device):
        return pltpu.make_async_remote_copy(
            src_ref=src, dst_ref=dst, send_sem=send, recv_sem=recv, device_id=device, device_id_type=MESH
        )

    def at_plane(k):
        p = peer(q, k, 4)
        return p, (g, 2 * z + p // 2, lax.rem(p, 2))

    def at_line(k):
        s = peer(z, k, depth)
        return s, (g, 2 * s + x, c)

    def at_row(k):
        s = peer(r, k, rows)
        return s, (g, s, c)

    def place(p):
        return pl.ds(pl.multiple_of(p * per, per), per)

    def side(p):
        return pl.ds(pl.multiple_of(p * pair, pair), pair)

    def share(d):
        return pl.ds(pl.multiple_of(d * some, some), some)

    loads = [
        pltpu.make_async_copy(t_hbm, t_ref, in_sem.at[0]),
        pltpu.make_async_copy(noise_hbm, noise_ref, in_sem.at[1]),
        pltpu.make_async_copy(e_ref, line.at[z], in_sem.at[2]),
        pltpu.make_async_copy(e_ref, plane.at[place(q)], in_sem.at[3]),
        pltpu.make_async_copy(t_hbm, tline.at[z], in_sem.at[4]),
    ]
    for load in loads:
        load.start()

    barrier = pltpu.get_barrier_semaphore()

    def greet(device):
        pl.semaphore_signal(barrier, inc=1, device_id=device, device_id_type=MESH)

    each(1, depth, lambda k: greet(at_line(k)[1]))
    each(1, 4, lambda k: greet(at_plane(k)[1]))
    pl.semaphore_wait(barrier, depth + 2)

    def e_line(k):
        return copy(e_ref, line.at[z], e_send.at[k], e_recv.at[z], at_line(k)[1])

    def e_plane(k):
        return copy(e_ref, plane.at[place(q)], b_send.at[k], b_recv.at[q], at_plane(k)[1])

    def t_row(k):
        return copy(t_hbm, tline.at[z], t_send.at[k], t_recv.at[z], at_line(k)[1])

    def t_from(k):
        s, device = at_line(k)
        return copy(t_hbm, tline.at[s], t_send.at[k], t_recv.at[s], device)

    def f_row(k):
        return copy(fall.at[r], fall.at[r], f_send.at[k], f_recv.at[r], at_row(k)[1])

    def f_from(k):
        s = at_row(k)[0]
        return copy(fall.at[s], fall.at[s], f_send.at[k], f_recv.at[s], at_row(k)[1])

    def p_plane(k):
        p, device = at_plane(k)
        return copy(part.at[1, :, side(p // 2)], pown.at[q], p_send.at[k], p_recv.at[q], device)

    def p_from(k):
        p, device = at_plane(k)
        return copy(pown.at[p], pown.at[p], p_send.at[k], p_recv.at[p], device)

    def between(i, src, dst):
        return copy(src, dst, s_send.at[i], s_recv.at[i], sibling)

    t_first = between(0, t_ref.at[share(other)], tsib)
    p_first = between(1, part.at[0, share(other)], psib)
    d_first = between(2, dall.at[c], dall.at[c])
    d_rest = between(3, rest.at[c], rest.at[c])

    each(1, depth, lambda k: t_row(depth - k).start())
    each(1, 4, lambda k: e_plane(4 - k).start())
    each(1, depth, lambda k: e_line(k).start())
    loads[0].wait()
    t_first.start()

    first = c == 0
    lane = lax.broadcasted_iota(jnp.int32, (count, pair), 1)
    row = lax.broadcasted_iota(jnp.int32, (count, pair), 0)
    spot = lax.broadcasted_iota(jnp.int32, (1, wide), 1) // per

    for load in loads[1:]:
        load.wait()
    noise = noise_ref[...]
    noise = jnp.where(spot == q, jnp.concatenate([noise] * 4, axis=1), 0.0)

    def b_arrived(k):
        p, device = at_plane(k)
        copy(e_ref, plane.at[place(p)], b_send.at[k], b_recv.at[p], device).wait_recv()

    each(1, 4, b_arrived)
    dims = (((1,), (1,)), ((), ()))
    block = plane[...]
    square = lax.dot_general(block, block, dims, preferred_element_type=f32)
    at = lax.broadcasted_iota(jnp.int32, square.shape, 0) == lax.broadcasted_iota(jnp.int32, square.shape, 1)
    row_norms = jnp.sum(jnp.where(at, square, 0.0), axis=0, keepdims=True) / width + 1e-05
    row_inverse = lax.rsqrt(row_norms)
    row_scale = row_norms * row_inverse / LAYERS
    row_inverse = row_inverse / width

    def gram(s):
        piece = line[s]
        sigma = lax.dot_general(piece, plane[...], dims, preferred_element_type=f32)
        values = piece.astype(f32)
        norms = jnp.sum(values * values, axis=1, keepdims=True) / width + 1e-05
        inverse = lax.rsqrt(norms)
        kernel = layers(sigma * inverse * row_inverse)
        kernel = kernel * (norms * inverse) * row_scale
        high = kernel.astype(bf16)
        khi[place(s), :] = high
        klo[place(s), :] = (kernel - high.astype(f32)).astype(bf16)

    gram(z)
    t_mine = t_ref[share(c), :]
    t_first.wait_recv()
    t_other = tsib[...]
    fall[r, :, wide:] = jnp.where(
        first, jnp.concatenate([t_mine, t_other], axis=1), jnp.concatenate([t_other, t_mine], axis=1)
    )
    each(1, depth, lambda k: t_from(k).wait_recv())
    vbuf[...] = jnp.concatenate([tline[k] for k in range(depth)], axis=1)

    def arrived(k):
        s, device = at_line(k)
        copy(e_ref, line.at[s], e_send.at[k], e_recv.at[s], device).wait_recv()
        gram(s)

    each(1, depth, arrived)

    def whole(ref, s, lanes):
        return jnp.concatenate([ref[0, s, :, lanes], ref[1, s, :, lanes]], axis=0)

    def columns(ref):
        for k in range(depth // 2):
            a, b = whole(ref, 2 * k, side(x)), whole(ref, 2 * k + 1, side(x))
            a = jnp.where(first, a, pltpu.roll(a, per, 1))
            b = jnp.where(first, pltpu.roll(b, per, 1), b)
            vbuf[:, pair * k : pair * (k + 1)] = jnp.where(lane < per, a, b)

    def apply(own):
        v = vbuf[...]
        high = v.astype(bf16)
        low = (v - high.astype(f32)).astype(bf16)
        both = jnp.concatenate([high, low], axis=0)
        a = jnp.dot(both, khi[...], preferred_element_type=f32)
        b = jnp.dot(high, klo[...], preferred_element_type=f32)
        return a[:count] + a[count:] + b + noise * own

    def total(values):
        return jnp.sum(jnp.sum(values, axis=0), axis=1, keepdims=True)

    own_targets = t_ref[...]
    part[0] = apply(jnp.concatenate([own_targets] * 4, axis=1))
    p_first.start()
    p_first.wait_recv()
    fall[r, :, :wide] = part[0, share(c), :] + psib[...]
    each(1, rows, lambda k: f_row(rows - k).start())
    each(1, rows, lambda k: f_from(k).wait_recv())
    held = fall[...].reshape(depth, 2, some, wide + pair)
    image = held[:, 0, :, :wide] + held[:, 1, :, :wide]
    targets = jnp.concatenate([held[:, 0, :, wide:], held[:, 1, :, wide:]], axis=2)
    norm_zero = total(targets * targets)
    alpha = norm_zero / total(targets * image)
    residual = targets - alpha[None] * image
    norm_one = total(residual * residual)
    beta = norm_one / norm_zero
    dall[c] = residual + beta[None] * targets
    d_first.start()
    even, odd = fall[2 * z], fall[2 * z + 1]
    image = even[:, :wide] + odd[:, :wide]
    rest[c, 0] = jnp.concatenate([even[:, wide:], odd[:, wide:]], axis=1) - alpha * image
    rest[c, 1] = jnp.broadcast_to(alpha, (some, wide))
    rest[c, 2] = jnp.broadcast_to(norm_one, (some, wide))
    d_rest.start()
    d_first.wait_recv()

    columns(dall)
    own_direction = whole(dall, z, slice(None))
    mine = apply(own_direction)
    curve = jnp.sum(own_direction * mine, axis=1, keepdims=True)
    me = 2 * r + c
    cbuf[me] = jnp.sum(jnp.where(lane == row, curve, 0.0), axis=0, keepdims=True)

    def everyone(step):
        def one(j):
            j = 2 * rows - j
            other_me = peer(me, j, 2 * rows)
            step(other_me // 2, lax.rem(other_me, 2), j)

        each(1, 2 * rows, one)

    def c_send_to(s, d, j):
        return copy(cbuf.at[me], cbuf.at[me], c_send.at[j], c_recv.at[me], (g, s, d))

    everyone(lambda s, d, j: c_send_to(s, d, j).start())
    part[1] = mine
    each(1, 4, lambda k: p_plane(k).start())
    pown[q] = part[1, :, side(x)]
    d_rest.wait_recv()

    def own(values):
        return jnp.where(first, values[:, :per], values[:, per:])

    def own_rest(i):
        return own(jnp.concatenate([rest[0, i, :, side(x)], rest[1, i, :, side(x)]], axis=0))

    own_residual, alpha, norm_one = own_rest(0), own_rest(1), own_rest(2)
    own_direction = own(whole(dall, z, side(x)))
    own_weights = alpha * own_targets
    each(1, 4, lambda k: p_from(k).wait_recv())
    own_image = own((pown[0] + pown[1]) + (pown[2] + pown[3]))
    everyone(
        lambda s, d, j: copy(
            cbuf.at[me], cbuf.at[2 * s + d], c_send.at[j], c_recv.at[2 * s + d], (g, s, d)
        ).wait_recv()
    )
    curve = jnp.sum(cbuf[...], axis=0)
    curve = jnp.sum(jnp.where(lane == row, curve, 0.0), axis=1, keepdims=True)
    step = norm_one / curve
    out_ref[0] = own_weights + step * own_direction
    out_ref[1] = own_residual - step * own_image

    for one in (t_first, p_first, d_first, d_rest):
        one.wait_send()

    def plane_sent(k):
        e_plane(k).wait_send()
        p_plane(k).wait_send()

    def line_sent(k):
        e_line(k).wait_send()
        t_row(k).wait_send()

    def row_sent(k):
        f_row(k).wait_send()

    each(1, 4, plane_sent)
    each(1, depth, line_sent)
    each(1, rows, row_sent)
    everyone(lambda s, d, j: c_send_to(s, d, j).wait_send())


def per_device(rows, embeddings, noise, targets):
    per, width = embeddings.shape
    count = targets.shape[0]
    some, depth, pair, wide = count // 2, rows // 2, 2 * per, 4 * per
    f32, bf16 = jnp.float32, jnp.bfloat16
    dma = pltpu.SemaphoreType.DMA
    vmem = pl.BlockSpec(memory_space=pltpu.VMEM)
    out = pl.pallas_call(
        functools.partial(body, rows),
        out_shape=jax.ShapeDtypeStruct((2, count, per), f32),
        in_specs=[pl.BlockSpec(memory_space=pltpu.HBM)] * 3,
        out_specs=vmem,
        scratch_shapes=[
            pltpu.VMEM((1, per), f32),
            pltpu.VMEM((count, per), f32),
            dma((5,)),
            pltpu.VMEM((depth, per, width), bf16),
            pltpu.VMEM((wide, width), bf16),
            pltpu.VMEM((some, per), f32),
            pltpu.VMEM((depth, count, per), f32),
            pltpu.VMEM((depth * per, wide), bf16),
            pltpu.VMEM((depth * per, wide), bf16),
            pltpu.VMEM((2, count, wide), f32),
            pltpu.VMEM((some, wide), f32),
            pltpu.VMEM((rows, some, wide + pair), f32),
            pltpu.VMEM((2, depth, some, wide), f32),
            pltpu.VMEM((2, 3, some, wide), f32),
            pltpu.VMEM((4, count, pair), f32),
            pltpu.VMEM((count, depth * per), f32),
            pltpu.VMEM((2 * rows, 1, pair), f32),
            dma((depth,)), dma((depth,)), dma((4,)), dma((4,)), dma((4,)), dma((4,)),
            dma((depth,)), dma((depth,)), dma((4,)), dma((4,)),
            dma((rows,)), dma((rows,)), dma((2 * rows,)), dma((2 * rows,)),
        ],
        compiler_params=pltpu.CompilerParams(
            collective_id=0, has_side_effects=True, vmem_limit_bytes=60 * 2**20
        ),
    )(embeddings, noise.reshape(1, per), targets)
    return out[0], out[1]


def solution(mesh):
    in_specs = (
        P(("groups", "col", "row"), None),
        P(("groups", "col", "row")),
        P(None, ("groups", "col", "row")),
    )
    out_specs = (P(None, ("groups", "col", "row")), P(None, ("groups", "col", "row")))
    return jax.shard_map(
        functools.partial(per_device, mesh.shape["row"]),
        mesh=mesh, in_specs=in_specs, out_specs=out_specs, check_vma=False,
    )
```

```python
import functools
import math

import jax
import jax.numpy as jnp
from jax import lax
from jax.experimental import pallas as pl
from jax.experimental.pallas import tpu as pltpu
from jax.sharding import PartitionSpec as P

LAYERS = 5
MESH = pl.DeviceIdType.MESH
ARCCOS = (
    1.5707963050,
    -0.2145988016,
    0.0889789874,
    -0.0501743046,
    0.0308918810,
    -0.0170881256,
    0.0066700901,
    -0.0012624911,
)


def each(start, stop, step):
    if stop - start <= 16:
        for k in range(start, stop):
            step(k)
    else:
        lax.fori_loop(start, stop, lambda k, _: (step(k), 0)[1], 0)


def peer(me, k, count):
    if count & (count - 1):
        return lax.rem(me + k, count)
    found, bit = 0, 1
    while bit < count:
        mine, turn = lax.rem(me // bit, 2), (k // bit) % 2
        found, bit = found + bit * (mine + turn - 2 * mine * turn), 2 * bit
    return found


def root(x):
    return x * lax.rsqrt(jnp.maximum(x, 1e-30))


def arccos_over_pi(x, root_one_minus):
    total = jnp.full_like(x, ARCCOS[-1] / math.pi)
    for coefficient in ARCCOS[-2::-1]:
        total = total * x + coefficient / math.pi
    return total * root_one_minus


def layers(first):
    rho = jnp.clip(first, -1.0, 1.0)
    kernel = first
    for layer in range(LAYERS - 1):
        size = jnp.abs(rho) if layer == 0 else rho
        rest = 1.0 - size
        angle = arccos_over_pi(size, root(rest))
        share = 1.0 - angle
        if layer == 0:
            share = jnp.where(rho < 0.0, angle, share)
        sigma = root(rest * (1.0 + size)) * (1.0 / math.pi) + share * rho
        kernel = sigma + kernel * share
        rho = jnp.minimum(sigma, 1.0)
    return kernel


def body(
    rows, e_ref, noise_hbm, t_hbm, out_ref,
    noise_ref, t_ref, in_sem, line, plane, tsib, tline, khi, klo, part, psib, fall, dall, rest, pown, vbuf, cbuf,
    e_send, e_recv, b_send, b_recv, s_send, s_recv, t_send, t_recv,
    p_send, p_recv, f_send, f_recv, c_send, c_recv,
):
    f32, bf16 = jnp.float32, jnp.bfloat16
    g, r, c = lax.axis_index("groups"), lax.axis_index("row"), lax.axis_index("col")
    per, width = e_ref.shape
    count = t_ref.shape[0]
    some = count // 2
    depth = rows // 2
    z, x = r // 2, lax.rem(r, 2)
    q = 2 * x + c
    pair, wide = 2 * per, 4 * per
    other = 1 - c
    sibling = (g, r, other)

    def copy(src, dst, send, recv, device):
        return pltpu.make_async_remote_copy(
            src_ref=src, dst_ref=dst, send_sem=send, recv_sem=recv, device_id=device, device_id_type=MESH
        )

    def at_plane(k):
        p = peer(q, k, 4)
        return p, (g, 2 * z + p // 2, lax.rem(p, 2))

    def at_line(k):
        s = peer(z, k, depth)
        return s, (g, 2 * s + x, c)

    def at_row(k):
        s = peer(r, k, rows)
        return s, (g, s, c)

    def place(p):
        return pl.ds(pl.multiple_of(p * per, per), per)

    def side(p):
        return pl.ds(pl.multiple_of(p * pair, pair), pair)

    def share(d):
        return pl.ds(pl.multiple_of(d * some, some), some)

    loads = [
        pltpu.make_async_copy(t_hbm, t_ref, in_sem.at[0]),
        pltpu.make_async_copy(noise_hbm, noise_ref, in_sem.at[1]),
        pltpu.make_async_copy(e_ref, line.at[z], in_sem.at[2]),
        pltpu.make_async_copy(e_ref, plane.at[place(q)], in_sem.at[3]),
        pltpu.make_async_copy(t_hbm, tline.at[z], in_sem.at[4]),
    ]
    barrier = pltpu.get_barrier_semaphore()

    def greet(device):
        pl.semaphore_signal(barrier, inc=1, device_id=device, device_id_type=MESH)

    each(1, depth, lambda k: greet(at_line(depth - k)[1]))
    each(1, 4, lambda k: greet(at_plane(4 - k)[1]))
    for load in loads:
        load.start()
    pl.semaphore_wait(barrier, depth + 2)

    def e_line(k):
        return copy(e_ref, line.at[z], e_send.at[k], e_recv.at[z], at_line(k)[1])

    def e_plane(k):
        return copy(e_ref, plane.at[place(q)], b_send.at[k], b_recv.at[q], at_plane(k)[1])

    def t_row(k):
        return copy(t_hbm, tline.at[z], t_send.at[k], t_recv.at[z], at_line(k)[1])

    def t_from(k):
        s, device = at_line(k)
        return copy(t_hbm, tline.at[s], t_send.at[k], t_recv.at[s], device)

    def f_row(k):
        return copy(fall.at[r], fall.at[r], f_send.at[k], f_recv.at[r], at_row(k)[1])

    def f_from(k):
        s = at_row(k)[0]
        return copy(fall.at[s], fall.at[s], f_send.at[k], f_recv.at[s], at_row(k)[1])

    def p_plane(k):
        p, device = at_plane(k)
        return copy(part.at[1, :, side(p // 2)], pown.at[q], p_send.at[k], p_recv.at[q], device)

    def p_from(k):
        p, device = at_plane(k)
        return copy(pown.at[p], pown.at[p], p_send.at[k], p_recv.at[p], device)

    def between(i, src, dst):
        return copy(src, dst, s_send.at[i], s_recv.at[i], sibling)

    t_first = between(0, t_ref.at[share(other)], tsib)
    p_first = between(1, part.at[0, share(other)], psib)
    d_first = between(2, dall.at[c], dall.at[c])
    d_rest = between(3, rest.at[c], rest.at[c])

    each(1, depth, lambda k: t_row(depth - k).start())
    each(1, 4, lambda k: e_plane(4 - k).start())
    each(1, depth, lambda k: e_line(k).start())
    loads[0].wait()
    t_first.start()

    first = c == 0
    lane = lax.broadcasted_iota(jnp.int32, (count, pair), 1)
    row = lax.broadcasted_iota(jnp.int32, (count, pair), 0)
    spot = lax.broadcasted_iota(jnp.int32, (1, wide), 1) // per

    for load in loads[1:]:
        load.wait()
    noise = noise_ref[...]
    noise = jnp.where(spot == q, jnp.concatenate([noise] * 4, axis=1), 0.0)

    def b_arrived(k):
        p, device = at_plane(k)
        copy(e_ref, plane.at[place(p)], b_send.at[k], b_recv.at[p], device).wait_recv()

    each(1, 4, b_arrived)
    dims = (((1,), (1,)), ((), ()))
    block = plane[...]
    square = lax.dot_general(block, block, dims, preferred_element_type=f32)
    at = lax.broadcasted_iota(jnp.int32, square.shape, 0) == lax.broadcasted_iota(jnp.int32, square.shape, 1)
    row_norms = jnp.sum(jnp.where(at, square, 0.0), axis=0, keepdims=True) / width + 1e-05
    row_inverse = lax.rsqrt(row_norms)
    row_scale = row_norms * row_inverse / LAYERS
    row_inverse = row_inverse / width

    def gram(s):
        piece = line[s]
        sigma = lax.dot_general(piece, plane[...], dims, preferred_element_type=f32)
        values = piece.astype(f32)
        norms = jnp.sum(values * values, axis=1, keepdims=True) / width + 1e-05
        inverse = lax.rsqrt(norms)
        kernel = layers(sigma * inverse * row_inverse)
        kernel = kernel * (norms * inverse) * row_scale
        high = kernel.astype(bf16)
        khi[place(s), :] = high
        klo[place(s), :] = (kernel - high.astype(f32)).astype(bf16)

    gram(z)
    t_mine = t_ref[share(c), :]
    t_first.wait_recv()
    t_other = tsib[...]
    fall[r, :, wide:] = jnp.where(
        first, jnp.concatenate([t_mine, t_other], axis=1), jnp.concatenate([t_other, t_mine], axis=1)
    )
    each(1, depth, lambda k: t_from(k).wait_recv())
    vbuf[...] = jnp.concatenate([tline[k] for k in range(depth)], axis=1)

    def arrived(k):
        s, device = at_line(k)
        copy(e_ref, line.at[s], e_send.at[k], e_recv.at[s], device).wait_recv()
        gram(s)

    each(1, depth, arrived)

    def whole(ref, s, lanes):
        return jnp.concatenate([ref[0, s, :, lanes], ref[1, s, :, lanes]], axis=0)

    def columns(ref):
        for k in range(depth // 2):
            a, b = whole(ref, 2 * k, side(x)), whole(ref, 2 * k + 1, side(x))
            a = jnp.where(first, a, pltpu.roll(a, per, 1))
            b = jnp.where(first, pltpu.roll(b, per, 1), b)
            vbuf[:, pair * k : pair * (k + 1)] = jnp.where(lane < per, a, b)

    def apply(own):
        v = vbuf[...]
        high = v.astype(bf16)
        low = (v - high.astype(f32)).astype(bf16)
        both = jnp.concatenate([high, low], axis=0)
        a = jnp.dot(both, khi[...], preferred_element_type=f32)
        b = jnp.dot(high, klo[...], preferred_element_type=f32)
        return a[:count] + a[count:] + b + noise * own

    def total(values):
        return jnp.sum(jnp.sum(values, axis=0), axis=1, keepdims=True)

    own_targets = t_ref[...]
    part[0] = apply(jnp.concatenate([own_targets] * 4, axis=1))
    p_first.start()
    p_first.wait_recv()
    fall[r, :, :wide] = part[0, share(c), :] + psib[...]
    each(1, rows, lambda k: f_row(rows - k).start())
    each(1, rows, lambda k: f_from(k).wait_recv())
    held = fall[...].reshape(depth, 2, some, wide + pair)
    image = held[:, 0, :, :wide] + held[:, 1, :, :wide]
    targets = jnp.concatenate([held[:, 0, :, wide:], held[:, 1, :, wide:]], axis=2)
    norm_zero = total(targets * targets)
    alpha = norm_zero / total(targets * image)
    residual = targets - alpha[None] * image
    norm_one = total(residual * residual)
    beta = norm_one / norm_zero
    dall[c] = residual + beta[None] * targets
    d_first.start()
    even, odd = fall[2 * z], fall[2 * z + 1]
    image = even[:, :wide] + odd[:, :wide]
    rest[c, 0] = jnp.concatenate([even[:, wide:], odd[:, wide:]], axis=1) - alpha * image
    rest[c, 1] = jnp.broadcast_to(alpha, (some, wide))
    rest[c, 2] = jnp.broadcast_to(norm_one, (some, wide))
    d_rest.start()
    d_first.wait_recv()

    columns(dall)
    own_direction = whole(dall, z, slice(None))
    mine = apply(own_direction)
    curve = jnp.sum(own_direction * mine, axis=1, keepdims=True)
    me = 2 * r + c
    cbuf[me] = jnp.sum(jnp.where(lane == row, curve, 0.0), axis=0, keepdims=True)

    def everyone(step):
        def one(j):
            j = 2 * rows - j
            other_me = peer(me, j, 2 * rows)
            step(other_me // 2, lax.rem(other_me, 2), j)

        each(1, 2 * rows, one)

    def c_send_to(s, d, j):
        return copy(cbuf.at[me], cbuf.at[me], c_send.at[j], c_recv.at[me], (g, s, d))

    everyone(lambda s, d, j: c_send_to(s, d, j).start())
    part[1] = mine
    each(1, 4, lambda k: p_plane(k).start())
    pown[q] = part[1, :, side(x)]
    d_rest.wait_recv()

    def own(values):
        return jnp.where(first, values[:, :per], values[:, per:])

    def own_rest(i):
        return own(jnp.concatenate([rest[0, i, :, side(x)], rest[1, i, :, side(x)]], axis=0))

    own_residual, alpha, norm_one = own_rest(0), own_rest(1), own_rest(2)
    own_direction = own(whole(dall, z, side(x)))
    own_weights = alpha * own_targets
    each(1, 4, lambda k: p_from(k).wait_recv())
    own_image = own((pown[0] + pown[1]) + (pown[2] + pown[3]))
    everyone(
        lambda s, d, j: copy(
            cbuf.at[me], cbuf.at[2 * s + d], c_send.at[j], c_recv.at[2 * s + d], (g, s, d)
        ).wait_recv()
    )
    curve = jnp.sum(cbuf[...], axis=0)
    curve = jnp.sum(jnp.where(lane == row, curve, 0.0), axis=1, keepdims=True)
    step = norm_one / curve
    out_ref[0] = own_weights + step * own_direction
    out_ref[1] = own_residual - step * own_image

    for one in (t_first, p_first, d_first, d_rest):
        one.wait_send()

    def plane_sent(k):
        e_plane(k).wait_send()
        p_plane(k).wait_send()

    def line_sent(k):
        e_line(k).wait_send()
        t_row(k).wait_send()

    def row_sent(k):
        f_row(k).wait_send()

    each(1, 4, plane_sent)
    each(1, depth, line_sent)
    each(1, rows, row_sent)
    everyone(lambda s, d, j: c_send_to(s, d, j).wait_send())


def per_device(rows, embeddings, noise, targets):
    per, width = embeddings.shape
    count = targets.shape[0]
    some, depth, pair, wide = count // 2, rows // 2, 2 * per, 4 * per
    f32, bf16 = jnp.float32, jnp.bfloat16
    dma = pltpu.SemaphoreType.DMA
    vmem = pl.BlockSpec(memory_space=pltpu.VMEM)
    out = pl.pallas_call(
        functools.partial(body, rows),
        out_shape=jax.ShapeDtypeStruct((2, count, per), f32),
        in_specs=[pl.BlockSpec(memory_space=pltpu.HBM)] * 3,
        out_specs=vmem,
        scratch_shapes=[
            pltpu.VMEM((1, per), f32),
            pltpu.VMEM((count, per), f32),
            dma((5,)),
            pltpu.VMEM((depth, per, width), bf16),
            pltpu.VMEM((wide, width), bf16),
            pltpu.VMEM((some, per), f32),
            pltpu.VMEM((depth, count, per), f32),
            pltpu.VMEM((depth * per, wide), bf16),
            pltpu.VMEM((depth * per, wide), bf16),
            pltpu.VMEM((2, count, wide), f32),
            pltpu.VMEM((some, wide), f32),
            pltpu.VMEM((rows, some, wide + pair), f32),
            pltpu.VMEM((2, depth, some, wide), f32),
            pltpu.VMEM((2, 3, some, wide), f32),
            pltpu.VMEM((4, count, pair), f32),
            pltpu.VMEM((count, depth * per), f32),
            pltpu.VMEM((2 * rows, 1, pair), f32),
            dma((depth,)), dma((depth,)), dma((4,)), dma((4,)), dma((4,)), dma((4,)),
            dma((depth,)), dma((depth,)), dma((4,)), dma((4,)),
            dma((rows,)), dma((rows,)), dma((2 * rows,)), dma((2 * rows,)),
        ],
        compiler_params=pltpu.CompilerParams(
            collective_id=0, has_side_effects=True, vmem_limit_bytes=60 * 2**20
        ),
    )(embeddings, noise.reshape(1, per), targets)
    return out[0], out[1]


def solution(mesh):
    in_specs = (
        P(("groups", "col", "row"), None),
        P(("groups", "col", "row")),
        P(None, ("groups", "col", "row")),
    )
    out_specs = (P(None, ("groups", "col", "row")), P(None, ("groups", "col", "row")))
    return jax.shard_map(
        functools.partial(per_device, mesh.shape["row"]),
        mesh=mesh, in_specs=in_specs, out_specs=out_specs, check_vma=False,
    )
```
